32 devices in a mesh: dp: 4 (over x, core), seq: 4 (over z), tensor: 2 (over y).
Axes of the slice: x: 2, y: 2, z: 4, core: 2. Of those that a mesh axis runs over, the one named last changes fastest.
Arguments:
- byte_acts: bfloat16 [4, 16384, 2048], P('dp', 'seq', 'tensor'), may hold values from -18 to 18
- conv_weight: bfloat16 [16, 1024, 128], P('tensor'), may hold values from -0.1875 to 0.1875
- conv_bias: float32 [2048], P('tensor'), may hold values from -3 to 3
- proj_weight: bfloat16 [2048, 8192], P(None, 'tensor'), may hold values from -0.125 to 0.125
- teacher: bfloat16 [4, 4096, 8192], P('dp', 'seq', 'tensor'), may hold values from -6 to 6
- span_lengths: int32 [4, 4096], P('dp'), may hold values from 1 to 16, as said below
Outputs:
- downsampled: bfloat16 [4, 4096, 2048], P('dp', 'seq', 'tensor')
- byte_grad: bfloat16 [4, 16384, 2048], P('dp', 'seq', 'tensor')
- conv_grad: float32 [16, 1024, 128], P('tensor')
- proj_grad: float32 [2048, 8192], P(None, 'tensor')
The draws below stay inside these ranges and needn't reach their ends.
Inputs may be any that keep to these rules, and one draw needn't show every extreme that they name: `span_lengths`: each document's 4096 span lengths cover its 16384 bytes in order; the longest is exactly 16.
All inputs are finite; a program needn't handle non-finite values.
Results may differ from the reference program's by a relative error of at most 0.019.
Values may be sent and summed in bfloat16 or wider, within the bound.
A program may use at most 256 MiB of HBM per device.

```python
import jax
import jax.numpy as jnp
from jax import lax

D = 2048
TD = 8192
GROUPS = 16
STRIDE = 4
KERNEL = 8
MOST_SPAN = 16
GW = 128
TD_DEV = 4096
DOCS = 4
SEQ_BYTES = 16384
POSITIONS = 4096
TOKENS = 4096


def draw_span_lengths(key, part):
    slot_tokens = TOKENS // 8
    key_long, key_cut, key_flip = jax.random.split(jax.random.fold_in(key, 7101), 3)
    long_len = jax.random.randint(key_long, (DOCS, 2, slot_tokens), 8, 14).astype(jnp.int32)
    long_len = long_len.at[:, 0, 0].set(MOST_SPAN).at[:, 1, 0].set(8)
    spare_bytes = 2 * MOST_SPAN - long_len[:, 0] - long_len[:, 1] - 6
    cut_points = jax.random.randint(key_cut, (DOCS, 5, slot_tokens), 0, 11).astype(jnp.int32)
    cut_points = jnp.minimum(cut_points, spare_bytes[:, None, :])
    cut_points = jnp.sort(cut_points, axis=1)
    edge_points = jnp.concatenate([jnp.zeros((DOCS, 1, slot_tokens), jnp.int32), cut_points, spare_bytes[:, None, :]], axis=1)
    short_len = 1 + edge_points[:, 1:] - edge_points[:, :-1]
    values = jnp.concatenate([long_len, short_len], axis=1)
    flip_bits = (jax.random.randint(key_flip, (), 0, 2) + jnp.arange(DOCS, dtype=jnp.int32)) % 2
    arranged = jnp.where(flip_bits[:, None, None] == 1, values[:, ::-1], values)
    return arranged.reshape(DOCS, TOKENS).astype(jnp.int32)


def draw_byte_acts(key, part):
    key_pair, key_value = jax.random.split(jax.random.fold_in(key, 5303), 2)
    pairing = jax.random.permutation(key_pair, DOCS).astype(jnp.int32)
    group_of = jnp.arange(D, dtype=jnp.int32) // GW % DOCS
    heavy = (group_of[None, :] == pairing[:, None]).astype(jnp.float32)
    factor = 1.0 + 2.0 * heavy
    base = jnp.clip(jax.random.normal(key_value, (DOCS, SEQ_BYTES, D), jnp.float32), -6.0, 6.0)
    return (base * factor[:, None, :]).astype(jnp.bfloat16)


def levels(own_key, shape, cuts, least, high):
    loudness = 1.0
    for dim, shards_of in cuts:
        heights = jax.random.uniform(jax.random.fold_in(jax.random.fold_in(own_key, 6), dim), (shards_of,), jnp.float32, least / len(cuts), high / len(cuts))
        loudness = loudness * jnp.repeat(jnp.exp(heights), shape[dim] // shards_of).reshape((-1,) + (1,) * (len(shape) - 1 - dim))
    return loudness


def scatter_about(own_key, extent, deviation, reach, cuts=(), held_as=jnp.bfloat16):
    entries = deviation * jax.random.normal(own_key, extent, jnp.float32)
    if cuts:
        entries = entries * levels(own_key, extent, cuts, -0.22, 0.18)
    return jnp.clip(entries, -reach, reach).astype(held_as)


def setup_inputs(seed: int = 0) -> dict:
    keys = jax.random.split(jax.random.key(seed), 7)
    byte_acts = draw_byte_acts(jax.random.fold_in(keys[6], 71), 0)
    conv_weight = scatter_about(keys[1], (GROUPS, KERNEL * GW, GW), (KERNEL * GW) ** -0.5, 0.1875, ((0, 2),))
    conv_bias = scatter_about(keys[2], (D,), 0.5, 3.0, ((0, 2),), jnp.float32)
    proj_weight = scatter_about(keys[3], (D, TD), D ** -0.5, 0.125, ((1, 2),))
    teacher = scatter_about(keys[4], (DOCS, TOKENS, TD), 1.0, 6.0, ((0, 4), (1, 4), (2, 2)))
    span_lengths = draw_span_lengths(jax.random.fold_in(keys[6], 71), 0)
    return dict(byte_acts=byte_acts, conv_weight=conv_weight, conv_bias=conv_bias, proj_weight=proj_weight, teacher=teacher, span_lengths=span_lengths)


def intersection_weights(span_start, span_end, span_lengths, first_position, position_count):
    byte_first = (first_position + jnp.arange(position_count, dtype=jnp.int32)) * STRIDE
    lower_edge = jnp.maximum(span_start[:, None], byte_first[None, :])
    upper_edge = jnp.minimum(span_end[:, None], byte_first[None, :] + STRIDE)
    covered = jnp.maximum(upper_edge - lower_edge, 0).astype(jnp.float32)
    return (covered / span_lengths[:, None].astype(jnp.float32)).astype(jnp.bfloat16)

def blockwise_back(err_grad, proj_weight):
    total = jnp.zeros((TOKENS, D), jnp.float32)
    for shard_index in range(TD // TD_DEV):
        err_part = err_grad[:, shard_index * TD_DEV:(shard_index + 1) * TD_DEV]
        weight_part = proj_weight[:, shard_index * TD_DEV:(shard_index + 1) * TD_DEV]
        partial_term = lax.dot_general(err_part, weight_part, (((1,), (1,)), ((), ())), preferred_element_type=jnp.float32)
        rounded = lax.optimization_barrier(partial_term.astype(jnp.bfloat16))
        total = total + rounded.astype(jnp.float32)
    return total.astype(jnp.bfloat16)

def reference(byte_acts, conv_weight, conv_bias, proj_weight, teacher, span_lengths):
    taps_weight = conv_weight.astype(jnp.float32).reshape(GROUPS, KERNEL, GW, GW)
    bias_groups = conv_bias.reshape(GROUPS, GW)
    proj_total = jnp.zeros((D, TD), jnp.float32)
    conv_total = jnp.zeros((GROUPS, KERNEL, GW, GW), jnp.float32)
    down_list = []
    grad_list = []
    for doc_index in range(DOCS):
        lengths_doc = span_lengths[doc_index].astype(jnp.int32)
        span_end = jnp.cumsum(lengths_doc).astype(jnp.int32)
        span_start = (span_end - lengths_doc).astype(jnp.int32)
        pool_weight = intersection_weights(span_start, span_end, lengths_doc, 0, POSITIONS)
        extended = jnp.concatenate([byte_acts[doc_index], jnp.zeros((STRIDE, D), byte_acts.dtype)], axis=0)
        blocks = extended.reshape(POSITIONS + 1, STRIDE, GROUPS, GW).astype(jnp.float32)
        windows = jnp.concatenate([blocks[:-1], blocks[1:]], axis=1)
        conv_out = jnp.einsum('pkgc,gkco->pgo', windows, taps_weight) + bias_groups[None]
        downsampled = conv_out.reshape(POSITIONS, D).astype(jnp.bfloat16)
        pooled = jnp.dot(pool_weight, downsampled, preferred_element_type=jnp.float32).astype(jnp.bfloat16)
        predicted = jnp.dot(pooled, proj_weight, preferred_element_type=jnp.float32)
        err_grad = (predicted - teacher[doc_index].astype(jnp.float32)).astype(jnp.bfloat16)
        proj_total = proj_total + jnp.dot(pooled.T, err_grad, preferred_element_type=jnp.float32)
        pooled_grad = blockwise_back(err_grad, proj_weight)
        down_grad = jnp.dot(pool_weight.T, pooled_grad, preferred_element_type=jnp.float32).astype(jnp.bfloat16)
        grad_groups = down_grad.astype(jnp.float32).reshape(POSITIONS, GROUPS, GW)
        conv_total = conv_total + jnp.einsum('pkgc,pgo->gkco', windows, grad_groups)
        window_grad = jnp.einsum('pgo,gkco->pkgc', grad_groups, taps_weight)
        block_grad = window_grad[:, :STRIDE]
        carried = jnp.concatenate([jnp.zeros((1, STRIDE, GROUPS, GW), jnp.float32), window_grad[:-1, STRIDE:]], axis=0)
        byte_doc = (block_grad + carried).reshape(SEQ_BYTES, D).astype(jnp.bfloat16)
        down_list.append(downsampled)
        grad_list.append(byte_doc)
    proj_grad = proj_total / jnp.sqrt(jnp.float32(DOCS * TOKENS))
    conv_grad = (conv_total / jnp.sqrt(jnp.float32(DOCS * POSITIONS))).reshape(GROUPS, KERNEL * GW, GW)
    return (jnp.stack(down_list), jnp.stack(grad_list), conv_grad, proj_grad)
```

```python
import jax
import jax.numpy as jnp
from jax import lax
from jax.sharding import PartitionSpec as P

STRIDE = 4
KERNEL = 8
FORWARD_CHUNKS = 2
BACKWARD_CHUNKS = 2
PROJ_CHUNKS = 2
F32 = jnp.float32
BF16 = jnp.bfloat16


def shifted(block, axis, distance):
    devices = range(lax.axis_size(axis))
    route = [(i - distance, i) for i in devices if i - distance in devices]
    return lax.ppermute(block, axis, route)


def ring(block, axis):
    count = lax.axis_size(axis)
    return lax.ppermute(block, axis, [(i, (i + 1) % count) for i in range(count)])


def swapped(block, axis, bit):
    count = lax.axis_size(axis)
    return lax.ppermute(block, axis, [(i, i ^ bit) for i in range(count)])


def prefix_sum(lengths):
    total = lengths.shape[0]
    cols = 128
    rows = total // cols
    table = lengths.reshape(rows, cols)
    col = jnp.arange(cols, dtype=jnp.int32)
    row = jnp.arange(rows, dtype=jnp.int32)
    inside = jnp.sum(
        jnp.where(col[None, :, None] >= col[None, None, :], table[:, None, :], 0), axis=2
    )
    row_total = jnp.sum(table, axis=1)
    before = jnp.sum(jnp.where(row[:, None] > row[None, :], row_total[None, :], 0), axis=1)
    return (inside + before[:, None]).reshape(total)


def intersection_weights(span_start, span_end, span_lengths, first_position, position_count):
    byte_first = (first_position + jnp.arange(position_count, dtype=jnp.int32)) * STRIDE
    lower_edge = jnp.maximum(span_start[:, None], byte_first[None, :])
    upper_edge = jnp.minimum(span_end[:, None], byte_first[None, :] + STRIDE)
    covered = jnp.maximum(upper_edge - lower_edge, 0).astype(F32)
    return (covered / span_lengths[:, None].astype(F32)).astype(BF16)


def halves(block, own):
    half = block.shape[0] // 2
    mine = lax.dynamic_slice_in_dim(block, own * half, half, 0)
    other = lax.dynamic_slice_in_dim(block, (1 - own) * half, half, 0)
    return mine, other


def rejoined(mine, other, own):
    return jnp.where(
        own == 0,
        jnp.concatenate([mine, other], axis=0),
        jnp.concatenate([other, mine], axis=0),
    )


def added(a, b):
    return (a.astype(F32) + b.astype(F32)).astype(BF16)


def summed_product(rows_t, right):
    dp_count = lax.axis_size("dp")
    dp_rank = lax.axis_index("dp")
    seq_count = lax.axis_size("seq")
    seq_rank = lax.axis_index("seq")
    bits = [1 << i for i in range(dp_count.bit_length() - 1)]

    def product(columns):
        return lax.dot_general(
            columns, right, (((0,), (0,)), ((), ())), preferred_element_type=F32
        )

    half = rows_t.shape[1] // 2
    own = dp_rank % 2
    send = product(lax.dynamic_slice_in_dim(rows_t, (1 - own) * half, half, 1)).astype(BF16)
    got = swapped(send, "dp", 1)
    mine = product(lax.dynamic_slice_in_dim(rows_t, own * half, half, 1))
    held = (mine + got.astype(F32)).astype(BF16)
    for bit in bits[1:]:
        keep, give = halves(held, dp_rank // bit % 2)
        held = added(keep, swapped(give, "dp", bit))
    depth = held.shape[0] // seq_count

    def part(index):
        return lax.dynamic_slice_in_dim(held, (index + seq_count) % seq_count * depth, depth, 0)

    moving = part(seq_rank - 1)
    for step in range(seq_count - 1):
        moving = added(ring(moving, "seq"), part(seq_rank - 2 - step))
    held = lax.all_gather(moving, "seq", axis=0, tiled=True)
    for bit in bits[::-1]:
        held = rejoined(held, swapped(held, "dp", bit), dp_rank // bit % 2)
    return held


def local(byte_acts, conv_weight, conv_bias, proj_weight, teacher, span_lengths):
    byte_rows = byte_acts[0]
    row_total, width = byte_rows.shape
    groups_here = conv_weight.shape[0]
    group_width = width // groups_here
    positions = row_total // STRIDE
    seq_count = lax.axis_size("seq")
    seq_rank = lax.axis_index("seq")
    dp_count = lax.axis_size("dp")
    tensor_count = lax.axis_size("tensor")
    tensor_rank = lax.axis_index("tensor")
    lengths_doc = span_lengths[0]
    tokens_all = lengths_doc.shape[0]
    tokens = tokens_all // seq_count
    span_end = prefix_sum(lengths_doc)
    span_start = span_end - lengths_doc

    def own_tokens(values):
        return lax.dynamic_slice_in_dim(values, seq_rank * tokens, tokens, 0)

    token_weight = intersection_weights(
        own_tokens(span_start),
        own_tokens(span_end),
        own_tokens(lengths_doc),
        0,
        positions * seq_count,
    )
    local_weight = intersection_weights(
        span_start, span_end, lengths_doc, seq_rank * positions, positions
    )

    next_rows = shifted(byte_rows[:STRIDE], "seq", -1)
    blocks = byte_rows.reshape(positions, STRIDE, groups_here, group_width)
    halo = next_rows.reshape(STRIDE, groups_here, group_width)
    taps = conv_weight.reshape(groups_here, 2, STRIDE, group_width, group_width)
    taps_pair = jnp.transpose(taps, (0, 2, 3, 1, 4)).reshape(
        groups_here, STRIDE, group_width, 2 * group_width
    )
    forward_chunks = min(FORWARD_CHUNKS, groups_here)
    backward_chunks = min(BACKWARD_CHUNKS, groups_here)

    per = groups_here // forward_chunks
    down_parts = []
    gathered_parts = []
    for chunk in range(forward_chunks):
        sel = slice(chunk * per, (chunk + 1) * per)
        both = jnp.einsum(
            "pkgc,gkcn->pgn", blocks[:, :, sel], taps_pair[sel], preferred_element_type=F32
        )
        tail = jnp.einsum(
            "kgc,gkco->go", halo[:, sel], taps[sel, 1], preferred_element_type=F32
        )
        later = jnp.concatenate([both[1:, :, group_width:], tail[None]], axis=0)
        bias = conv_bias.reshape(groups_here, group_width)[sel]
        part = both[:, :, :group_width] + later + bias[None]
        part = part.reshape(positions, per * group_width).astype(BF16)
        down_parts.append(part)
        whole = lax.all_gather(part, "seq", axis=0, tiled=True)
        pooled = jnp.dot(token_weight, whole, preferred_element_type=F32).astype(BF16)
        gathered_parts.append(lax.all_gather(pooled, "tensor", axis=1, tiled=False))
    downsampled = jnp.concatenate(down_parts, axis=1)
    gathered = jnp.concatenate(gathered_parts, axis=2).reshape(tokens, tensor_count * width)

    predicted = jnp.dot(gathered, proj_weight, preferred_element_type=F32)
    err_grad = (predicted - teacher[0].astype(F32)).astype(BF16)

    weight_blocks = proj_weight.reshape(tensor_count, width, proj_weight.shape[1])
    per = groups_here // backward_chunks
    span = per * group_width
    token_grads = []
    for chunk in range(backward_chunks):
        weight_part = weight_blocks[:, chunk * span : (chunk + 1) * span]
        if tensor_count == 2:
            def back(block):
                return lax.dot_general(
                    lax.dynamic_index_in_dim(weight_part, block, 0, keepdims=False),
                    err_grad,
                    (((1,), (1,)), ((), ())),
                    preferred_element_type=F32,
                ).astype(BF16)

            got = swapped(back(1 - tensor_rank), "tensor", 1)
            pooled_grad_t = added(back(tensor_rank), got)
        else:
            pooled_grad_t = lax.psum_scatter(
                lax.dot_general(
                    weight_part.reshape(tensor_count * span, -1),
                    err_grad,
                    (((1,), (1,)), ((), ())),
                    preferred_element_type=F32,
                ).astype(BF16),
                "tensor",
                scatter_dimension=0,
                tiled=True,
            )
        token_grads.append(lax.all_gather(pooled_grad_t, "seq", axis=1, tiled=True))

    chunk_rows = gathered.shape[1] // PROJ_CHUNKS
    token_scale = 1.0 / jnp.sqrt(F32(dp_count * tokens_all))
    proj_parts = [
        summed_product(gathered[:, i * chunk_rows : (i + 1) * chunk_rows], err_grad)
        for i in range(PROJ_CHUNKS)
    ]

    position_scale = 1.0 / jnp.sqrt(F32(dp_count * positions * seq_count))
    byte_parts = []
    conv_parts = []
    for chunk in range(backward_chunks):
        sel = slice(chunk * per, (chunk + 1) * per)
        down = lax.dot_general(
            local_weight,
            token_grads[chunk],
            (((0,), (1,)), ((), ())),
            preferred_element_type=F32,
        ).astype(BF16)
        before = shifted(down[-1:], "seq", 1)
        earlier = jnp.concatenate([before, down[:-1]], axis=0)
        pair = jnp.concatenate(
            [
                down.reshape(positions, per, group_width),
                earlier.reshape(positions, per, group_width),
            ],
            axis=2,
        )
        grads = jnp.einsum(
            "pkgc,pgn->gkcn", blocks[:, :, sel], pair, preferred_element_type=F32
        )
        grads = grads.reshape(per, STRIDE, group_width, 2, group_width)
        conv_parts.append(jnp.transpose(grads, (0, 3, 1, 2, 4)))
        part = jnp.einsum(
            "pgn,gkcn->pkgc", pair, taps_pair[sel], preferred_element_type=F32
        )
        byte_parts.append(part.astype(BF16))
    byte_grad = jnp.concatenate(byte_parts, axis=2).reshape(row_total, width)
    conv_local = jnp.concatenate(conv_parts, axis=0)
    conv_summed = lax.psum(conv_local.astype(BF16), ("dp", "seq")).astype(F32)
    conv_grad = (conv_summed * position_scale).reshape(
        groups_here, KERNEL * group_width, group_width
    )
    proj_grad = jnp.concatenate([p.astype(F32) * token_scale for p in proj_parts], axis=0)
    return (downsampled[None], byte_grad[None], conv_grad, proj_grad)


def solution(mesh):
    return jax.shard_map(
        local,
        mesh=mesh,
        in_specs=(
            P("dp", "seq", "tensor"),
            P("tensor", None, None),
            P("tensor"),
            P(None, "tensor"),
            P("dp", "seq", "tensor"),
            P("dp", None),
        ),
        out_specs=(
            P("dp", "seq", "tensor"),
            P("dp", "seq", "tensor"),
            P("tensor", None, None),
            P(None, "tensor"),
        ),
        check_vma=False,
    )
```

```python
import jax
import jax.numpy as jnp
from jax import lax
from jax.sharding import PartitionSpec as P

STRIDE = 4
KERNEL = 8
FORWARD_CHUNKS = 2
BACKWARD_CHUNKS = 2
PROJ_CHUNKS = 2
F32 = jnp.float32
BF16 = jnp.bfloat16


def shifted(block, axis, distance):
    devices = range(lax.axis_size(axis))
    route = [(i - distance, i) for i in devices if i - distance in devices]
    return lax.ppermute(block, axis, route)


def swapped(block, axis, bit):
    count = lax.axis_size(axis)
    return lax.ppermute(block, axis, [(i, i ^ bit) for i in range(count)])


def prefix_sum(lengths):
    total = lengths.shape[0]
    cols = 128
    rows = total // cols
    table = lengths.reshape(rows, cols)
    col = jnp.arange(cols, dtype=jnp.int32)
    row = jnp.arange(rows, dtype=jnp.int32)
    inside = jnp.sum(
        jnp.where(col[None, :, None] >= col[None, None, :], table[:, None, :], 0), axis=2
    )
    row_total = jnp.sum(table, axis=1)
    before = jnp.sum(jnp.where(row[:, None] > row[None, :], row_total[None, :], 0), axis=1)
    return (inside + before[:, None]).reshape(total)


def intersection_weights(span_start, span_end, span_lengths, first_position, position_count):
    byte_first = (first_position + jnp.arange(position_count, dtype=jnp.int32)) * STRIDE
    lower_edge = jnp.maximum(span_start[:, None], byte_first[None, :])
    upper_edge = jnp.minimum(span_end[:, None], byte_first[None, :] + STRIDE)
    covered = jnp.maximum(upper_edge - lower_edge, 0).astype(F32)
    return (covered / span_lengths[:, None].astype(F32)).astype(BF16)


def halves(block, own):
    half = block.shape[0] // 2
    mine = lax.dynamic_slice_in_dim(block, own * half, half, 0)
    other = lax.dynamic_slice_in_dim(block, (1 - own) * half, half, 0)
    return mine, other


def rejoined(mine, other, own):
    return jnp.where(
        own == 0,
        jnp.concatenate([mine, other], axis=0),
        jnp.concatenate([other, mine], axis=0),
    )


def added(a, b):
    return (a.astype(F32) + b.astype(F32)).astype(BF16)


def bit_list(axis):
    return [1 << i for i in range(lax.axis_size(axis).bit_length() - 1)]


def product(columns, right):
    return lax.dot_general(
        columns, right, (((0,), (0,)), ((), ())), preferred_element_type=F32
    )


def column_half(rows_t, which):
    half = rows_t.shape[1] // 2
    return lax.dynamic_slice_in_dim(rows_t, which * half, half, 1)


def summed_rest(held):
    dp_rank = lax.axis_index("dp")
    bits = bit_list("dp")[1:]
    for bit in bits:
        keep, give = halves(held, dp_rank // bit % 2)
        held = added(keep, swapped(give, "dp", bit))
    held = lax.psum(held, "seq")
    for bit in bits[::-1]:
        held = rejoined(held, swapped(held, "dp", bit), dp_rank // bit % 2)
    return held


def local(byte_acts, conv_weight, conv_bias, proj_weight, teacher, span_lengths):
    byte_rows = byte_acts[0]
    row_total, width = byte_rows.shape
    groups_here = conv_weight.shape[0]
    group_width = width // groups_here
    positions = row_total // STRIDE
    seq_count = lax.axis_size("seq")
    seq_rank = lax.axis_index("seq")
    dp_count = lax.axis_size("dp")
    tensor_count = lax.axis_size("tensor")
    tensor_rank = lax.axis_index("tensor")
    lengths_doc = span_lengths[0]
    tokens_all = lengths_doc.shape[0]
    tokens = tokens_all // seq_count
    span_end = prefix_sum(lengths_doc)
    span_start = span_end - lengths_doc

    def own_tokens(values):
        return lax.dynamic_slice_in_dim(values, seq_rank * tokens, tokens, 0)

    token_weight = intersection_weights(
        own_tokens(span_start),
        own_tokens(span_end),
        own_tokens(lengths_doc),
        0,
        positions * seq_count,
    )
    local_weight = intersection_weights(
        span_start, span_end, lengths_doc, seq_rank * positions, positions
    )

    next_rows = shifted(byte_rows[:STRIDE], "seq", -1)
    blocks = byte_rows.reshape(positions, STRIDE, groups_here, group_width)
    halo = next_rows.reshape(STRIDE, groups_here, group_width)
    taps = conv_weight.reshape(groups_here, 2, STRIDE, group_width, group_width)
    taps_pair = jnp.transpose(taps, (0, 2, 3, 1, 4)).reshape(
        groups_here, STRIDE, group_width, 2 * group_width
    )
    forward_chunks = min(FORWARD_CHUNKS, groups_here)
    backward_chunks = min(BACKWARD_CHUNKS, groups_here)

    per = groups_here // forward_chunks
    down_parts = []
    gathered_parts = []
    pooled_parts = []
    got_parts = []
    for chunk in range(forward_chunks):
        sel = slice(chunk * per, (chunk + 1) * per)
        both = jnp.einsum(
            "pkgc,gkcn->pgn", blocks[:, :, sel], taps_pair[sel], preferred_element_type=F32
        )
        tail = jnp.einsum(
            "kgc,gkco->go", halo[:, sel], taps[sel, 1], preferred_element_type=F32
        )
        later = jnp.concatenate([both[1:, :, group_width:], tail[None]], axis=0)
        bias = conv_bias.reshape(groups_here, group_width)[sel]
        part = both[:, :, :group_width] + later + bias[None]
        part = part.reshape(positions, per * group_width).astype(BF16)
        down_parts.append(part)
        whole = lax.all_gather(part, "seq", axis=0, tiled=True)
        pooled = jnp.dot(token_weight, whole, preferred_element_type=F32).astype(BF16)
        if tensor_count == 2:
            got = swapped(pooled, "tensor", 1)
            pooled_parts.append(pooled)
            got_parts.append(got)
        else:
            gathered_parts.append(lax.all_gather(pooled, "tensor", axis=1, tiled=False))
    downsampled = jnp.concatenate(down_parts, axis=1)
    if tensor_count == 2:
        gathered = jnp.where(
            tensor_rank == 0,
            jnp.concatenate(pooled_parts + got_parts, axis=1),
            jnp.concatenate(got_parts + pooled_parts, axis=1),
        )
    else:
        gathered = jnp.concatenate(gathered_parts, axis=2)
        gathered = gathered.reshape(tokens, tensor_count * width)

    predicted = jnp.dot(gathered, proj_weight, preferred_element_type=F32)
    err_grad = (predicted - teacher[0].astype(F32)).astype(BF16)

    weight_blocks = proj_weight.reshape(tensor_count, width, proj_weight.shape[1])
    per = groups_here // backward_chunks
    span = per * group_width
    token_grads = []
    for chunk in range(backward_chunks):
        weight_part = weight_blocks[:, chunk * span : (chunk + 1) * span]
        if tensor_count == 2:
            def back(block):
                return lax.dot_general(
                    lax.dynamic_index_in_dim(weight_part, block, 0, keepdims=False),
                    err_grad,
                    (((1,), (1,)), ((), ())),
                    preferred_element_type=F32,
                ).astype(BF16)

            got = swapped(back(1 - tensor_rank), "tensor", 1)
            pooled_grad_t = added(back(tensor_rank), got)
        else:
            pooled_grad_t = lax.psum_scatter(
                lax.dot_general(
                    weight_part.reshape(tensor_count * span, -1),
                    err_grad,
                    (((1,), (1,)), ((), ())),
                    preferred_element_type=F32,
                ).astype(BF16),
                "tensor",
                scatter_dimension=0,
                tiled=True,
            )
        token_grads.append(pooled_grad_t)

    dp_rank = lax.axis_index("dp")
    own = dp_rank % 2
    chunk_rows = gathered.shape[1] // PROJ_CHUNKS
    token_scale = 1.0 / jnp.sqrt(F32(dp_count * tokens_all))
    chunks = [gathered[:, i * chunk_rows : (i + 1) * chunk_rows] for i in range(PROJ_CHUNKS)]
    sends = [product(column_half(c, 1 - own), err_grad).astype(BF16) for c in chunks]
    sends, token_grads = lax.optimization_barrier((sends, token_grads))
    token_grads = [lax.all_gather(t, "seq", axis=1, tiled=True) for t in token_grads]
    proj_grad = jnp.zeros((gathered.shape[1], err_grad.shape[1]), F32)
    for i in range(PROJ_CHUNKS):
        mine = product(column_half(chunks[i], own), err_grad)
        held = (mine + swapped(sends[i], "dp", 1).astype(F32)).astype(BF16)
        held = summed_rest(held)
        other = swapped(held, "dp", 1)
        for block, which in ((held, own), (other, 1 - own)):
            proj_grad = lax.dynamic_update_slice_in_dim(
                proj_grad,
                block.astype(F32) * token_scale,
                i * chunk_rows + which * (chunk_rows // 2),
                0,
            )

    position_scale = 1.0 / jnp.sqrt(F32(dp_count * positions * seq_count))
    down_parts = [
        lax.dot_general(
            local_weight, whole, (((0,), (1,)), ((), ())), preferred_element_type=F32
        ).astype(BF16)
        for whole in token_grads
    ]
    down = jnp.concatenate(down_parts, axis=1)
    before = shifted(down[-1:], "seq", 1)
    earlier = jnp.concatenate([before, down[:-1]], axis=0)
    pair = jnp.concatenate(
        [
            down.reshape(positions, groups_here, group_width),
            earlier.reshape(positions, groups_here, group_width),
        ],
        axis=2,
    )
    grads = jnp.einsum("pkgc,pgn->gkcn", blocks, pair, preferred_element_type=F32)
    grads = grads.astype(BF16).reshape(-1, 2 * group_width)
    keep, give = halves(grads, own)
    held = summed_rest(added(keep, swapped(give, "dp", 1)))
    grads = rejoined(held, swapped(held, "dp", 1), own).astype(F32) * position_scale
    grads = grads.reshape(groups_here, STRIDE, group_width, 2, group_width)
    conv_grad = jnp.transpose(grads, (0, 3, 1, 2, 4)).reshape(
        groups_here, KERNEL * group_width, group_width
    )
    byte_grad = jnp.einsum(
        "pgn,gkcn->pkgc", pair, taps_pair, preferred_element_type=F32
    ).astype(BF16).reshape(row_total, width)
    return (downsampled[None], byte_grad[None], conv_grad, proj_grad)


def solution(mesh):
    return jax.shard_map(
        local,
        mesh=mesh,
        in_specs=(
            P("dp", "seq", "tensor"),
            P("tensor", None, None),
            P("tensor"),
            P(None, "tensor"),
            P("dp", "seq", "tensor"),
            P("dp", None),
        ),
        out_specs=(
            P("dp", "seq", "tensor"),
            P("dp", "seq", "tensor"),
            P("tensor", None, None),
            P(None, "tensor"),
        ),
        check_vma=False,
    )
```
